32 devices in a mesh: rows: 4 (over z), segment: 4 (over y, x), tm: 2 (over core).
Axes of the slice: x: 2, y: 2, z: 4, core: 2. Of those that a mesh axis runs over, the one named last changes fastest.
Arguments:
- latents: bfloat16 [4, 8, 8, 128, 128], P(None, 'tm', 'rows'), may hold values from -40 to 40
- conv_first: bfloat16 [4, 3, 3, 3, 128, 128], P('segment'), may hold values from -0.109375 to 0.109375
- conv_second: bfloat16 [4, 3, 3, 3, 128, 128], P('segment'), may hold values from -0.109375 to 0.109375
- gain_first: bfloat16 [4, 128], P('segment'), may hold values from 0.099609375 to 1.8984375
- bias_first: bfloat16 [4, 128], P('segment'), may hold values from -1 to 1
- gain_second: bfloat16 [4, 128], P('segment'), may hold values from 0.099609375 to 1.8984375
- bias_second: bfloat16 [4, 128], P('segment'), may hold values from -1 to 1
Outputs:
- decoded: bfloat16 [4, 8, 8, 128, 128], P('segment', 'tm', 'rows')
The draws below stay inside these ranges and needn't reach their ends.
All inputs are finite; a program needn't handle non-finite values.
Results may differ from the reference program's by a relative error of at most 0.022.
Values may be sent and summed in bfloat16 or wider, within the bound.
A program may use at most 64 MiB of HBM per device.

```python
import jax
import jax.numpy as jnp
from jax import lax

C = 128
GROUPS = 32
F = 4
W = 128
MICRO = 4
FRAMES = 8
HEIGHT = 8
LAYERS = 4
N_TM = 2


def draw_latents(key, part):
    key_base, key_rows, key_cols, key_amp, key_spread, key_offset = jax.random.split(key, 6)
    shape = (MICRO, FRAMES, HEIGHT, W, C)
    row_scale = jnp.exp(jax.random.uniform(key_rows, (MICRO, HEIGHT), jnp.float32, -1.1513, 1.1513))
    col_scale = jnp.exp(jax.random.uniform(key_cols, (MICRO, W), jnp.float32, -1.1513, 1.1513))
    amplitude = jnp.exp(jax.random.uniform(key_amp, (MICRO,), jnp.float32, -1.1513, 1.1513))
    spread = jax.random.uniform(key_spread, (MICRO,), jnp.float32, 0.0, 3.0)
    offset = jax.random.normal(key_offset, (MICRO, C), jnp.float32) * spread[:, None]
    heights = jnp.arange(HEIGHT, dtype=jnp.float32) / HEIGHT - 0.5
    rising = jnp.exp(heights * 1.0986123)
    base = jax.random.normal(key_base, shape, jnp.float32)
    base = base + offset[:, None, None, None, :]
    factor = (row_scale * rising[None, :])[:, None, :, None, None] * col_scale[:, None, None, :, None]
    factor = factor * amplitude[:, None, None, None, None] * 0.05
    return jnp.clip(base * factor, -40.0, 40.0).astype(jnp.bfloat16)


def shard_levels(own_key, shape, cuts, low, high):
    def one(dim, parts):
        draws = jax.random.uniform(jax.random.fold_in(jax.random.fold_in(own_key, 6), dim), (parts,), jnp.float32, low / len(cuts), high / len(cuts))
        return jnp.repeat(jnp.exp(draws), shape[dim] // parts).reshape((-1,) + (1,) * (len(shape) - dim - 1))

    factor_of = one(*cuts[0])
    for cut in cuts[1:]:
        factor_of = factor_of * one(*cut)
    return factor_of


def noise(key, dims, scale, reach, cuts=(), kind=jnp.bfloat16):
    values = scale * jax.random.normal(key, dims, jnp.float32)
    if cuts:
        values = values * shard_levels(key, dims, cuts, -0.22, 0.18)
    return jnp.clip(values, -reach, reach).astype(kind)


def setup_inputs(seed: int = 0) -> dict:
    arg_keys = jax.random.split(jax.random.key(seed), 8)
    latents = draw_latents(jax.random.fold_in(arg_keys[7], 71), 0)
    conv_first = noise(arg_keys[1], (LAYERS, 3, 3, 3, C, C), (27 * C) ** -0.5, 0.109375, ((0, 4),))
    conv_second = noise(arg_keys[2], (LAYERS, 3, 3, 3, C, C), (27 * C) ** -0.5, 0.109375, ((0, 4),))
    gain_first = jnp.clip(1.0 + 0.18 * jax.random.normal(arg_keys[3], (LAYERS, C), jnp.float32), 0.099609375, 1.8984375).astype(jnp.bfloat16)
    bias_first = jnp.clip(jax.random.uniform(arg_keys[4], (LAYERS, C), jnp.float32, -1.0, 1.0) * shard_levels(arg_keys[4], (LAYERS, C), ((0, 4),), -0.4, 0.0), -1.0, 1.0).astype(jnp.bfloat16)
    gain_second = jnp.clip(1.0 + 0.18 * jax.random.normal(arg_keys[5], (LAYERS, C), jnp.float32), 0.099609375, 1.8984375).astype(jnp.bfloat16)
    bias_second = jnp.clip(jax.random.uniform(arg_keys[6], (LAYERS, C), jnp.float32, -1.0, 1.0) * shard_levels(arg_keys[6], (LAYERS, C), ((0, 4),), -0.4, 0.0), -1.0, 1.0).astype(jnp.bfloat16)
    return dict(latents=latents, conv_first=conv_first, conv_second=conv_second, gain_first=gain_first, bias_first=bias_first, gain_second=gain_second, bias_second=bias_second)


EPS = 1e-06

def normalize(values, norm_gain, norm_bias):
    width_group = C // GROUPS
    grouped = values.astype(jnp.float32).reshape(N_TM, F, HEIGHT, W, GROUPS, width_group)
    members = F * HEIGHT * W * width_group
    average = lax.optimization_barrier(jnp.sum(grouped, axis=(1, 2, 3, 5))) / members
    squares = lax.optimization_barrier(jnp.sum(grouped * grouped, axis=(1, 2, 3, 5))) / members
    inverse = lax.rsqrt(squares - average * average + EPS)
    scaled = (grouped - average[:, None, None, None, :, None]) * inverse[:, None, None, None, :, None]
    scaled = scaled.reshape(values.shape) * norm_gain.astype(jnp.float32) + norm_bias.astype(jnp.float32)
    return jax.nn.silu(scaled).astype(jnp.bfloat16)

def convolve(active, kernel):
    result = lax.conv_general_dilated(active[None], kernel, (1, 1, 1), ((2, 0), (1, 1), (1, 1)), dimension_numbers=('NDHWC', 'DHWIO', 'NDHWC'), preferred_element_type=jnp.float32)
    return result[0]

def reference(latents, conv_first, conv_second, gain_first, bias_first, gain_second, bias_second):

    def decode(values):
        for layer_index in range(LAYERS):
            active = normalize(values, gain_first[layer_index], bias_first[layer_index])
            hidden = convolve(active, conv_first[layer_index]).astype(jnp.bfloat16)
            active = normalize(hidden, gain_second[layer_index], bias_second[layer_index])
            values = (values.astype(jnp.float32) + convolve(active, conv_second[layer_index])).astype(jnp.bfloat16)
        return values
    return lax.map(decode, latents)
```

```python
import jax
import jax.numpy as jnp
from jax import lax
from jax.sharding import PartitionSpec as P

GROUPS = 32


EPS = 1e-06


def passed_along(value, axis, steps):
    count = lax.axis_size(axis)
    initial, last = (max(0, -steps), min(count, count - steps))
    return lax.ppermute(value, axis, [(source, source + steps) for source in range(initial, last)])


def padded_2(block, sides, width):
    for axis, dim in sides:
        count = lax.axis_size(axis)
        forward = [(i, i + 1) for i in range(count - 1)]
        backward = [(target, source) for source, target in forward]
        low = lax.ppermute(
            lax.slice_in_dim(block, block.shape[dim] - width, None, axis=dim), axis, forward
        )
        high = lax.ppermute(lax.slice_in_dim(block, 0, width, axis=dim), axis, backward)
        block = jnp.concatenate([low, block, high], axis=dim)
    return block


def normalize(values, norm_gain, norm_bias):
    frames, rows_here, columns, channels = values.shape
    width_group = channels // GROUPS
    grouped = values.astype(jnp.float32).reshape(frames, rows_here, columns, GROUPS, width_group)
    totals = lax.psum(
        (jnp.sum(grouped, axis=(0, 1, 2, 4)), jnp.sum(grouped * grouped, axis=(0, 1, 2, 4))), "rows"
    )
    members = frames * rows_here * lax.axis_size("rows") * columns * width_group
    average = totals[0] / members
    squares = totals[1] / members
    inverse = lax.rsqrt(squares - average * average + EPS)
    scaled = (grouped - average[:, None]) * inverse[:, None]
    scaled = scaled.reshape(values.shape) * norm_gain.astype(jnp.float32) + norm_bias.astype(
        jnp.float32
    )
    return jax.nn.silu(scaled).astype(jnp.bfloat16)


def convolve(active, kernel):
    previous = passed_along(active[-2:], "tm", 1)
    extended = jnp.concatenate([previous, active], axis=0)
    padded = padded_2(extended, (("rows", 1),), 1)
    padded = jnp.pad(padded, ((0, 0), (0, 0), (1, 1), (0, 0)))
    result = lax.conv_general_dilated(
        padded[None],
        kernel,
        (1, 1, 1),
        "VALID",
        dimension_numbers=("NDHWC", "DHWIO", "NDHWC"),
        preferred_element_type=jnp.float32,
    )
    return result[0]


def residual_block(values, params):
    first, second, gain_one, bias_one, gain_two, bias_two = params
    active = normalize(values, gain_one, bias_one)
    hidden = convolve(active, first).astype(jnp.bfloat16)
    active = normalize(hidden, gain_two, bias_two)
    return (values.astype(jnp.float32) + convolve(active, second)).astype(jnp.bfloat16)


def body(latents, conv_first, conv_second, gain_first, bias_first, gain_second, bias_second):
    segments = lax.axis_size("segment")
    micro = latents.shape[0]
    per_segment = micro // segments
    position = lax.axis_index("segment")
    small = jnp.stack([gain_first, bias_first, gain_second, bias_second], axis=1)
    small = lax.all_gather(small, "segment", axis=0, tiled=True)
    first = lax.all_gather(conv_first, "segment", axis=0, tiled=True)
    second = lax.all_gather(conv_second, "segment", axis=0, tiled=True)
    outs = []
    for index in range(per_segment):
        values = lax.dynamic_index_in_dim(
            latents, position * per_segment + index, 0, keepdims=False
        )
        for layer in range(first.shape[0]):
            gains = small[layer]
            values = residual_block(
                values, (first[layer], second[layer], gains[0], gains[1], gains[2], gains[3])
            )
        outs.append(values)
    return jnp.stack(outs)


def solution(mesh):
    in_specs = (
        P(None, "tm", "rows", None, None),
        P("segment", None, None, None, None, None),
        P("segment", None, None, None, None, None),
        P("segment", None),
        P("segment", None),
        P("segment", None),
        P("segment", None),
    )
    out_specs = P("segment", "tm", "rows", None, None)
    return jax.shard_map(body, mesh=mesh, in_specs=in_specs, out_specs=out_specs, check_vma=False)
```

```python
import functools

import jax
import jax.numpy as jnp
from jax import lax
from jax.experimental import pallas as pl
from jax.experimental.pallas import tpu as pltpu
from jax.sharding import PartitionSpec as P

GROUPS = 32


EPS = 1e-06


def passed_along(value, axis, steps):
    count = lax.axis_size(axis)
    initial, last = (max(0, -steps), min(count, count - steps))
    return lax.ppermute(value, axis, [(source, source + steps) for source in range(initial, last)])


def padded_2(block, sides, width):
    for axis, dim in sides:
        count = lax.axis_size(axis)
        forward = [(i, i + 1) for i in range(count - 1)]
        backward = [(target, source) for source, target in forward]
        low = lax.ppermute(
            lax.slice_in_dim(block, block.shape[dim] - width, None, axis=dim), axis, forward
        )
        high = lax.ppermute(lax.slice_in_dim(block, 0, width, axis=dim), axis, backward)
        block = jnp.concatenate([low, block, high], axis=dim)
    return block


def normalize(values, norm_gain, norm_bias):
    frames, rows_here, columns, channels = values.shape
    width_group = channels // GROUPS
    grouped = values.astype(jnp.float32).reshape(frames, rows_here, columns, GROUPS, width_group)
    totals = lax.psum(
        (jnp.sum(grouped, axis=(0, 1, 2, 4)), jnp.sum(grouped * grouped, axis=(0, 1, 2, 4))), "rows"
    )
    members = frames * rows_here * lax.axis_size("rows") * columns * width_group
    average = totals[0] / members
    squares = totals[1] / members
    inverse = lax.rsqrt(squares - average * average + EPS)
    scaled = (grouped - average[:, None]) * inverse[:, None]
    scaled = scaled.reshape(values.shape) * norm_gain.astype(jnp.float32) + norm_bias.astype(
        jnp.float32
    )
    return jax.nn.silu(scaled).astype(jnp.bfloat16)


def convolve(active, kernel):
    previous = passed_along(active[-2:], "tm", 1)
    extended = jnp.concatenate([previous, active], axis=0)
    padded = padded_2(extended, (("rows", 1),), 1)
    padded = jnp.pad(padded, ((0, 0), (0, 0), (1, 1), (0, 0)))
    result = lax.conv_general_dilated(
        padded[None],
        kernel,
        (1, 1, 1),
        "VALID",
        dimension_numbers=("NDHWC", "DHWIO", "NDHWC"),
        preferred_element_type=jnp.float32,
    )
    return result[0]


def residual_block(values, params):
    first, second, gain_one, bias_one, gain_two, bias_two = params
    active = normalize(values, gain_one, bias_one)
    hidden = convolve(active, first).astype(jnp.bfloat16)
    active = normalize(hidden, gain_two, bias_two)
    return (values.astype(jnp.float32) + convolve(active, second)).astype(jnp.bfloat16)


def body(latents, conv_first, conv_second, gain_first, bias_first, gain_second, bias_second):
    segments = lax.axis_size("segment")
    micro = latents.shape[0]
    per_segment = micro // segments
    position = lax.axis_index("segment")
    small = jnp.stack([gain_first, bias_first, gain_second, bias_second], axis=1)
    small = lax.all_gather(small, "segment", axis=0, tiled=True)
    first = lax.all_gather(conv_first, "segment", axis=0, tiled=True)
    second = lax.all_gather(conv_second, "segment", axis=0, tiled=True)
    outs = []
    for index in range(per_segment):
        values = lax.dynamic_index_in_dim(
            latents, position * per_segment + index, 0, keepdims=False
        )
        for layer in range(first.shape[0]):
            gains = small[layer]
            values = residual_block(
                values, (first[layer], second[layer], gains[0], gains[1], gains[2], gains[3])
            )
        outs.append(values)
    return jnp.stack(outs)


MESH = pl.DeviceIdType.MESH
TILE = 16
PIECES = 2


def fused(
    latents, first, second, small, out,
    wbuf, gbuf, vin, values, raw, padded, act, edge_out, edge_in, stat_out, stat_in,
    in_send, in_recv, own_sem, w_send, w_recv, w_own, g_send, g_recv,
    e_send, e_recv, s_send, s_recv, o_send, o_recv,
):
    rows_count = lax.axis_size("rows")
    cores = lax.axis_size("tm")
    group = rows_count * cores
    segments = lax.axis_size("segment")
    z = lax.axis_index("rows")
    core = lax.axis_index("tm")
    seg = lax.axis_index("segment")
    me = z * cores + core
    _, frames_here, rows_here, _, channels = latents.shape
    frames = frames_here * cores
    height = rows_here * rows_count
    lines = frames * height
    taps = first.shape[0]
    half = taps // 2
    piece = half // PIECES
    span_size = frames_here * height * TILE
    convs = 2 * segments
    across = seg + 1 - 2 * lax.rem(seg, 2)
    along = lax.rem(seg + 2, 4)

    def member(c):
        return {"rows": c // cores, "tm": lax.rem(c, cores)}

    partners = [lax.rem(me + d, group) for d in range(1, group)]
    others = [lax.rem(seg + d, segments) for d in range(1, segments)]

    barrier = pltpu.get_barrier_semaphore()
    for c in partners:
        pl.semaphore_signal(barrier, inc=1, device_id=member(c), device_id_type=MESH)
    for s in others:
        pl.semaphore_signal(barrier, inc=1, device_id={"segment": s}, device_id_type=MESH)
    pl.semaphore_wait(barrier, group - 1 + segments - 1)

    def start_owner(i, source):
        k = 2 * seg + i
        for q in range(PIECES):
            rows = pl.ds(core * half + q * piece, piece)
            for slot, target in enumerate((across, along)):
                pltpu.make_async_remote_copy(
                    source.at[rows], wbuf.at[k, rows],
                    w_send.at[k, q, slot], w_recv.at[k, core, q],
                    device_id={"segment": target}, device_id_type=MESH,
                ).start()

    start_owner(0, first)

    def input_copy(c, sender):
        dst = vin.at[
            pl.ds(lax.rem(sender, cores) * frames_here, frames_here),
            pl.ds((sender // cores) * rows_here, rows_here),
        ]
        src = latents.at[seg, :, :, pl.ds(c * TILE, TILE)]
        return src, dst

    for c in partners:
        src, dst = input_copy(c, me)
        pltpu.make_async_remote_copy(
            src, dst, in_send.at[c], in_recv.at[me], device_id=member(c), device_id_type=MESH
        ).start()
    src, dst = input_copy(me, me)
    own = pltpu.make_async_copy(src, dst, own_sem)
    own.start()

    for s in others:
        pltpu.make_async_remote_copy(
            small, gbuf.at[seg], g_send.at[s], g_recv.at[seg],
            device_id={"segment": s}, device_id_type=MESH,
        ).start()
    gbuf[seg] = small[...]

    for i, source in enumerate((first, second)):
        pltpu.make_async_copy(source, wbuf.at[2 * seg + i], w_own.at[i]).start()
    start_owner(1, second)

    act[...] = jnp.zeros_like(act)
    padded[...] = jnp.zeros_like(padded)

    def relation(k):
        block = k // 2
        low = lax.rem(lax.rem(seg, 2) + lax.rem(block, 2), 2)
        high = lax.rem(seg // 2 + block // 2, 2)
        return low + 2 * high

    def landed(k, part, q):
        rows = pl.ds(part * half + q * piece, piece)
        return pltpu.make_async_remote_copy(
            wbuf.at[k, rows], wbuf.at[k, rows], w_send.at[k, q, 2], w_recv.at[k, part, q],
            device_id={"tm": 1 - core}, device_id_type=MESH,
        )

    def forwarded(k, q):
        rows = pl.ds(core * half + q * piece, piece)
        target = jnp.where(core == 0, along, across)
        return pltpu.make_async_remote_copy(
            wbuf.at[k, rows], wbuf.at[k, rows], w_send.at[k, q, 0], w_recv.at[k, core, q],
            device_id={"segment": target}, device_id_type=MESH,
        )

    def pump(k):
        kind = relation(k)
        for q in range(PIECES):

            @pl.when(kind != 0)
            def _():
                landed(k, core, q).wait_recv()

                @pl.when(kind == core + 1)
                def _():
                    forwarded(k, q).start()

                landed(k, core, q).start()

    def arrive(k):
        kind = relation(k)

        @pl.when(kind != 0)
        def _():
            for q in range(PIECES):
                landed(k, 1 - core, q).wait_recv()

        @pl.when(kind == 0)
        def _():
            i = lax.rem(k, 2)
            pltpu.make_async_copy(first, wbuf.at[k], w_own.at[i]).wait()

    def put(k, span, fresh):
        raw[pl.ds(span * span_size, span_size)] = fresh
        total = jnp.sum(fresh, axis=0, keepdims=True)
        squares = jnp.sum(fresh * fresh, axis=0, keepdims=True)
        which = lax.broadcasted_iota(jnp.int32, (8, channels), 0)
        stat_out[k, span] = jnp.where(which == 0, total, jnp.where(which == 1, squares, 0.0))

    def edge_copy(k, side):
        target = jnp.where(side == 0, me - 1, me + 1)
        return pltpu.make_async_remote_copy(
            edge_out.at[k, side], edge_in.at[k, 1 - side],
            e_send.at[k, side], e_recv.at[k, 1 - side],
            device_id=member(target), device_id_type=MESH,
        )

    def edge_wait(k, side):
        return pltpu.make_async_remote_copy(
            edge_out.at[k, side], edge_in.at[k, side],
            e_send.at[k, side], e_recv.at[k, side],
            device_id=member(jnp.where(side == 0, me - 1, me + 1)), device_id_type=MESH,
        )

    has = (me > 0, me < group - 1)

    def stat_copy(k, c, slot):
        return pltpu.make_async_remote_copy(
            stat_out.at[k], stat_in.at[k, slot], s_send.at[k, c], s_recv.at[k, slot],
            device_id=member(c), device_id_type=MESH,
        )

    def publish(k):
        for side, column in ((0, 0), (1, TILE - 1)):
            edge_out[k, side] = raw[pl.ds(column, lines, stride=TILE), :].astype(jnp.bfloat16)
        for c in partners:
            stat_copy(k, c, me).start()
        for side in (0, 1):

            @pl.when(has[side])
            def _():
                edge_copy(k, side).start()

        stat_in[k, me] = stat_out[k]

    def group_sum(t):
        lane = lax.broadcasted_iota(jnp.int32, t.shape, 1)
        width = t.shape[1]
        size = 1
        while size < width // GROUPS:
            up = pltpu.roll(t, width - size, 1)
            down = pltpu.roll(t, size, 1)
            t = t + jnp.where(lax.rem(lane // size, 2) == 0, up, down)
            size *= 2
        return t

    members = frames_here * height * TILE * group * (channels // GROUPS)

    def normalize_span(k, span):
        block = k // 2
        which = lax.rem(k, 2)
        total = stat_in[k, 0, span]
        for c in range(1, group):
            total = total + stat_in[k, c, span]
        total = group_sum(total)
        average = total[0:1] / members
        squares = total[1:2] / members
        inverse = lax.rsqrt(squares - average * average + EPS)
        params = gbuf[block]
        gain = jnp.where(which == 0, params[0:1], params[2:3])
        bias = jnp.where(which == 0, params[1:2], params[3:4])
        scale = inverse * gain

        def active(u):
            y = (u - average) * scale + bias
            return 0.5 * y * (1.0 + jnp.tanh(0.5 * y))

        count = frames_here * height
        flat = padded.reshape(lines * 2 * TILE, channels)
        for side, column in ((0, 7), (1, 8 + TILE)):

            @pl.when(has[side])
            def _():
                u = edge_in[k, side, pl.ds(span * count, count)].astype(jnp.float32)
                flat[pl.ds(span * count * 2 * TILE + column, count, stride=2 * TILE), :] = active(u)

        for f in range(frames_here):
            frame = span * frames_here + f
            u = raw[pl.ds(frame * height * TILE, height * TILE)]
            here = pl.ds(frame * height, height)
            y = active(u).reshape(height, TILE, channels)
            padded[here, 8 : 8 + TILE] = y
            for dx in range(3):
                shifted = y if dx == 1 else padded[here, 7 + dx : 7 + dx + TILE]
                act[frame + 2, 1 : height + 1, :, dx * channels : (dx + 1) * channels] = (
                    shifted.astype(jnp.bfloat16)
                )

    def convolve_span(k, span):
        total = None
        for dt in range(3):
            columns = [
                act[pl.ds(span * frames_here + dt, frames_here), dy : dy + height].reshape(
                    span_size, 3 * channels
                )
                for dy in range(3)
            ]
            x = jnp.concatenate(columns, axis=1)
            w = wbuf[k, dt * (taps // 3) : (dt + 1) * (taps // 3)]
            part = jnp.dot(x, w, preferred_element_type=jnp.float32)
            total = part if total is None else total + part
        return total

    def phase(k):
        publish(k)

        @pl.when(k <= 2)
        def _():
            pump(k)

        @pl.when(jnp.logical_and(k >= 2, k + 1 < convs))
        def _():
            pump(k + 1)

        for c in partners:
            stat_copy(k, c, c).wait_recv()
        for side in (0, 1):

            @pl.when(has[side])
            def _():
                edge_wait(k, side).wait_recv()

        for span in range(cores):
            normalize_span(k, span)
        arrive(k)

    for c in partners:
        src, dst = input_copy(me, c)
        pltpu.make_async_remote_copy(
            src, dst, in_send.at[c], in_recv.at[c], device_id=member(c), device_id_type=MESH
        ).wait_recv()
    own.wait()
    for span in range(cores):
        fresh = vin[span * frames_here : (span + 1) * frames_here]
        fresh = fresh.reshape(span_size, channels).astype(jnp.float32)
        values[span * span_size : (span + 1) * span_size] = fresh
        put(0, span, fresh)
    for s in others:
        pltpu.make_async_remote_copy(
            small, gbuf.at[s], g_send.at[s], g_recv.at[s],
            device_id={"segment": s}, device_id_type=MESH,
        ).wait_recv()

    @pl.loop(0, segments)
    def _(block):
        k = 2 * block
        phase(k)

        @pl.loop(0, cores)
        def _(span):
            hidden = convolve_span(k, span)
            put(k + 1, span, hidden.astype(jnp.bfloat16).astype(jnp.float32))

        phase(k + 1)

        @pl.loop(0, cores)
        def _(span):
            here = pl.ds(span * span_size, span_size)
            fresh = values[here] + convolve_span(k + 1, span)
            fresh = fresh.astype(jnp.bfloat16)
            values[here] = fresh.astype(jnp.float32)
            vin[pl.ds(span * frames_here, frames_here)] = fresh.reshape(
                frames_here, height, TILE, channels
            )
            put(k + 2, span, fresh.astype(jnp.float32))

    def output_copy(c, sender):
        src = vin.at[
            pl.ds(lax.rem(c, cores) * frames_here, frames_here),
            pl.ds((c // cores) * rows_here, rows_here),
        ]
        return src, out.at[:, :, pl.ds(sender * TILE, TILE)]

    for c in partners:
        src, dst = output_copy(c, me)
        pltpu.make_async_remote_copy(
            src, dst, o_send.at[c], o_recv.at[me], device_id=member(c), device_id_type=MESH
        ).start()
    src, dst = output_copy(me, me)
    own = pltpu.make_async_copy(src, dst, own_sem)
    own.start()

    for c in partners:
        src, dst = input_copy(c, me)
        pltpu.make_async_remote_copy(
            src, dst, in_send.at[c], in_recv.at[me], device_id=member(c), device_id_type=MESH
        ).wait_send()
    for s in others:
        pltpu.make_async_remote_copy(
            small, gbuf.at[seg], g_send.at[s], g_recv.at[seg],
            device_id={"segment": s}, device_id_type=MESH,
        ).wait_send()
    for i, source in enumerate((first, second)):
        k = 2 * seg + i
        for q in range(PIECES):
            rows = pl.ds(core * half + q * piece, piece)
            for slot, target in enumerate((across, along)):
                pltpu.make_async_remote_copy(
                    source.at[rows], wbuf.at[k, rows],
                    w_send.at[k, q, slot], w_recv.at[k, core, q],
                    device_id={"segment": target}, device_id_type=MESH,
                ).wait_send()

    @pl.loop(0, convs)
    def _(k):
        kind = relation(k)
        for q in range(PIECES):

            @pl.when(kind != 0)
            def _():
                landed(k, core, q).wait_send()

            @pl.when(kind == core + 1)
            def _():
                forwarded(k, q).wait_send()

        for c in partners:
            stat_copy(k, c, me).wait_send()
        for side in (0, 1):

            @pl.when(has[side])
            def _():
                edge_copy(k, side).wait_send()

    own.wait()
    for c in partners:
        src, dst = output_copy(me, c)
        copy = pltpu.make_async_remote_copy(
            src, dst, o_send.at[c], o_recv.at[c], device_id=member(c), device_id_type=MESH
        )
        copy.wait_recv()
        src, dst = output_copy(c, me)
        pltpu.make_async_remote_copy(
            src, dst, o_send.at[c], o_recv.at[me], device_id=member(c), device_id_type=MESH
        ).wait_send()


def in_one_kernel(
    latents, conv_first, conv_second, gain_first, bias_first, gain_second, bias_second
):
    segments = lax.axis_size("segment")
    cores = lax.axis_size("tm")
    group = lax.axis_size("rows") * cores
    micro, frames_here, rows_here, columns, channels = latents.shape
    frames, height = frames_here * cores, rows_here * lax.axis_size("rows")
    lines, pixels = frames * height, frames * height * TILE
    convs = 2 * segments
    taps = 27 * channels
    small = jnp.concatenate([gain_first, bias_first, gain_second, bias_second])
    small = jnp.pad(small.astype(jnp.float32), ((0, 4), (0, 0)))
    dma = pltpu.SemaphoreType.DMA
    any_space = pl.BlockSpec(memory_space=pl.ANY)
    vmem = pl.BlockSpec(memory_space=pltpu.VMEM)
    result = pl.pallas_call(
        fused,
        out_shape=jax.ShapeDtypeStruct((frames_here, rows_here, columns, channels), jnp.bfloat16),
        in_specs=[any_space] * 3 + [vmem],
        out_specs=any_space,
        scratch_shapes=[
            pltpu.VMEM((convs, taps, channels), jnp.bfloat16),
            pltpu.VMEM((segments, 8, channels), jnp.float32),
            pltpu.VMEM((frames, height, TILE, channels), jnp.bfloat16),
            pltpu.VMEM((pixels, channels), jnp.float32),
            pltpu.VMEM((pixels, channels), jnp.float32),
            pltpu.VMEM((lines, 2 * TILE, channels), jnp.float32),
            pltpu.VMEM((frames + 2, height + 2, TILE, 3 * channels), jnp.bfloat16),
            pltpu.VMEM((convs, 2, lines, channels), jnp.bfloat16),
            pltpu.VMEM((convs, 2, lines, channels), jnp.bfloat16),
            pltpu.VMEM((convs + 1, cores, 8, channels), jnp.float32),
            pltpu.VMEM((convs, group, cores, 8, channels), jnp.float32),
            dma((group,)), dma((group,)), dma,
            dma((convs, PIECES, 3)), dma((convs, 2, PIECES)), dma((2,)),
            dma((segments,)), dma((segments,)),
            dma((convs, 2)), dma((convs, 2)),
            dma((convs, group)), dma((convs, group)),
            dma((group,)), dma((group,)),
        ],
        compiler_params=pltpu.CompilerParams(
            collective_id=0, has_side_effects=True, vmem_limit_bytes=40 * 1024 * 1024
        ),
        cost_estimate=pl.CostEstimate(
            flops=2 * convs * pixels * taps * channels,
            bytes_accessed=6 * taps * channels,
            transcendentals=convs * pixels * channels,
        ),
    )(latents, conv_first.reshape(taps, channels), conv_second.reshape(taps, channels), small)
    return result[None]


def choose(latents, *params):
    cores = lax.axis_size("tm")
    group = lax.axis_size("rows") * cores
    fits = (
        lax.axis_size("segment") == 4
        and latents.shape[0] == 4
        and cores == 2
        and latents.shape[3] == group * TILE
    )
    return in_one_kernel(latents, *params) if fits else body(latents, *params)


def solution(mesh):
    in_specs = (
        P(None, "tm", "rows", None, None),
        P("segment", None, None, None, None, None),
        P("segment", None, None, None, None, None),
        P("segment", None),
        P("segment", None),
        P("segment", None),
        P("segment", None),
    )
    out_specs = P("segment", "tm", "rows", None, None)
    return jax.shard_map(choose, mesh=mesh, in_specs=in_specs, out_specs=out_specs, check_vma=False)
```

```python
import functools

import jax
import jax.numpy as jnp
from jax import lax
from jax.experimental import pallas as pl
from jax.experimental.pallas import tpu as pltpu
from jax.sharding import PartitionSpec as P

GROUPS = 32


EPS = 1e-06


def passed_along(value, axis, steps):
    count = lax.axis_size(axis)
    initial, last = (max(0, -steps), min(count, count - steps))
    return lax.ppermute(value, axis, [(source, source + steps) for source in range(initial, last)])


def padded_2(block, sides, width):
    for axis, dim in sides:
        count = lax.axis_size(axis)
        forward = [(i, i + 1) for i in range(count - 1)]
        backward = [(target, source) for source, target in forward]
        low = lax.ppermute(
            lax.slice_in_dim(block, block.shape[dim] - width, None, axis=dim), axis, forward
        )
        high = lax.ppermute(lax.slice_in_dim(block, 0, width, axis=dim), axis, backward)
        block = jnp.concatenate([low, block, high], axis=dim)
    return block


def normalize(values, norm_gain, norm_bias):
    frames, rows_here, columns, channels = values.shape
    width_group = channels // GROUPS
    grouped = values.astype(jnp.float32).reshape(frames, rows_here, columns, GROUPS, width_group)
    totals = lax.psum(
        (jnp.sum(grouped, axis=(0, 1, 2, 4)), jnp.sum(grouped * grouped, axis=(0, 1, 2, 4))), "rows"
    )
    members = frames * rows_here * lax.axis_size("rows") * columns * width_group
    average = totals[0] / members
    squares = totals[1] / members
    inverse = lax.rsqrt(squares - average * average + EPS)
    scaled = (grouped - average[:, None]) * inverse[:, None]
    scaled = scaled.reshape(values.shape) * norm_gain.astype(jnp.float32) + norm_bias.astype(
        jnp.float32
    )
    return jax.nn.silu(scaled).astype(jnp.bfloat16)


def convolve(active, kernel):
    previous = passed_along(active[-2:], "tm", 1)
    extended = jnp.concatenate([previous, active], axis=0)
    padded = padded_2(extended, (("rows", 1),), 1)
    padded = jnp.pad(padded, ((0, 0), (0, 0), (1, 1), (0, 0)))
    result = lax.conv_general_dilated(
        padded[None],
        kernel,
        (1, 1, 1),
        "VALID",
        dimension_numbers=("NDHWC", "DHWIO", "NDHWC"),
        preferred_element_type=jnp.float32,
    )
    return result[0]


def residual_block(values, params):
    first, second, gain_one, bias_one, gain_two, bias_two = params
    active = normalize(values, gain_one, bias_one)
    hidden = convolve(active, first).astype(jnp.bfloat16)
    active = normalize(hidden, gain_two, bias_two)
    return (values.astype(jnp.float32) + convolve(active, second)).astype(jnp.bfloat16)


def body(latents, conv_first, conv_second, gain_first, bias_first, gain_second, bias_second):
    segments = lax.axis_size("segment")
    micro = latents.shape[0]
    per_segment = micro // segments
    position = lax.axis_index("segment")
    small = jnp.stack([gain_first, bias_first, gain_second, bias_second], axis=1)
    small = lax.all_gather(small, "segment", axis=0, tiled=True)
    first = lax.all_gather(conv_first, "segment", axis=0, tiled=True)
    second = lax.all_gather(conv_second, "segment", axis=0, tiled=True)
    outs = []
    for index in range(per_segment):
        values = lax.dynamic_index_in_dim(
            latents, position * per_segment + index, 0, keepdims=False
        )
        for layer in range(first.shape[0]):
            gains = small[layer]
            values = residual_block(
                values, (first[layer], second[layer], gains[0], gains[1], gains[2], gains[3])
            )
        outs.append(values)
    return jnp.stack(outs)


MESH = pl.DeviceIdType.MESH
TILE = 16
PIECES = 3


def fused(
    latents, first, second, small, out,
    wbuf, gbuf, vin, values, raw, padded, act, edge_out, edge_in, stat_out, stat_in,
    in_send, in_recv, own_sem, w_send, w_recv, w_own, g_send, g_recv,
    e_send, e_recv, s_send, s_recv, o_send, o_recv,
):
    rows_count = lax.axis_size("rows")
    cores = lax.axis_size("tm")
    group = rows_count * cores
    segments = lax.axis_size("segment")
    z = lax.axis_index("rows")
    core = lax.axis_index("tm")
    seg = lax.axis_index("segment")
    me = z * cores + core
    _, frames_here, rows_here, _, channels = latents.shape
    frames = frames_here * cores
    height = rows_here * rows_count
    lines = frames * height
    taps = first.shape[0]
    half = taps // 2
    piece = half // PIECES
    span_size = frames_here * height * TILE
    convs = 2 * segments
    across = seg + 1 - 2 * lax.rem(seg, 2)
    along = lax.rem(seg + 2, 4)

    def member(c):
        return {"rows": c // cores, "tm": lax.rem(c, cores)}

    order = sorted(range(1, group), key=lambda d: -min(d, group - d))
    partners = [lax.rem(me + d, group) for d in order]
    others = [lax.rem(seg + d, segments) for d in range(1, segments)]

    barrier = pltpu.get_barrier_semaphore()
    for c in partners:
        pl.semaphore_signal(barrier, inc=1, device_id=member(c), device_id_type=MESH)
    for s in others:
        pl.semaphore_signal(barrier, inc=1, device_id={"segment": s}, device_id_type=MESH)
    pl.semaphore_wait(barrier, group - 1 + segments - 1)

    def start_owner(i, source):
        k = 2 * seg + i
        for q in range(PIECES):
            rows = pl.ds(core * half + q * piece, piece)
            for slot, target in enumerate((across, along)):
                pltpu.make_async_remote_copy(
                    source.at[rows], wbuf.at[k, rows],
                    w_send.at[k, q, slot], w_recv.at[k, core, q],
                    device_id={"segment": target}, device_id_type=MESH,
                ).start()

    start_owner(0, first)

    def input_copy(c, sender):
        dst = vin.at[
            pl.ds(lax.rem(sender, cores) * frames_here, frames_here),
            pl.ds((sender // cores) * rows_here, rows_here),
        ]
        src = latents.at[seg, :, :, pl.ds(c * TILE, TILE)]
        return src, dst

    for c in partners:
        src, dst = input_copy(c, me)
        pltpu.make_async_remote_copy(
            src, dst, in_send.at[c], in_recv.at[me], device_id=member(c), device_id_type=MESH
        ).start()
    src, dst = input_copy(me, me)
    own = pltpu.make_async_copy(src, dst, own_sem)
    own.start()

    for s in others:
        pltpu.make_async_remote_copy(
            small, gbuf.at[seg], g_send.at[s], g_recv.at[seg],
            device_id={"segment": s}, device_id_type=MESH,
        ).start()
    gbuf[seg] = small[...]

    for i, source in enumerate((first, second)):
        pltpu.make_async_copy(source, wbuf.at[2 * seg + i], w_own.at[i]).start()
    start_owner(1, second)

    act[...] = jnp.zeros_like(act)
    padded[...] = jnp.zeros_like(padded)

    def relation(k):
        block = k // 2
        low = lax.rem(lax.rem(seg, 2) + lax.rem(block, 2), 2)
        high = lax.rem(seg // 2 + block // 2, 2)
        return low + 2 * high

    def landed(k, part, q):
        rows = pl.ds(part * half + q * piece, piece)
        return pltpu.make_async_remote_copy(
            wbuf.at[k, rows], wbuf.at[k, rows], w_send.at[k, q, 2], w_recv.at[k, part, q],
            device_id={"tm": 1 - core}, device_id_type=MESH,
        )

    def forwarded(k, q):
        rows = pl.ds(core * half + q * piece, piece)
        target = jnp.where(core == 0, along, across)
        return pltpu.make_async_remote_copy(
            wbuf.at[k, rows], wbuf.at[k, rows], w_send.at[k, q, 0], w_recv.at[k, core, q],
            device_id={"segment": target}, device_id_type=MESH,
        )

    def pump(k):
        kind = relation(k)
        for q in range(PIECES):

            @pl.when(kind != 0)
            def _():
                landed(k, core, q).wait_recv()

                @pl.when(kind == core + 1)
                def _():
                    forwarded(k, q).start()

                landed(k, core, q).start()

    def arrive(k):
        kind = relation(k)

        @pl.when(kind != 0)
        def _():
            for q in range(PIECES):
                landed(k, 1 - core, q).wait_recv()

        @pl.when(kind == 0)
        def _():
            i = lax.rem(k, 2)
            pltpu.make_async_copy(first, wbuf.at[k], w_own.at[i]).wait()

    def put(k, span, fresh):
        raw[pl.ds(span * span_size, span_size)] = fresh
        total = jnp.sum(fresh, axis=0, keepdims=True)
        squares = jnp.sum(fresh * fresh, axis=0, keepdims=True)
        stat_out[k, span] = jnp.concatenate([total, squares], axis=0)

    count = frames_here * height

    def edge_copy(k, side, span, landing):
        return pltpu.make_async_remote_copy(
            edge_out.at[k, side, span], edge_in.at[k, landing, span],
            e_send.at[k, side, span], e_recv.at[k, landing, span],
            device_id=member(me - 1 if side == 0 else me + 1), device_id_type=MESH,
        )

    has = (me > 0, me < group - 1)

    def stat_copy(k, span, c, slot):
        return pltpu.make_async_remote_copy(
            stat_out.at[k, span], stat_in.at[k, slot, span],
            s_send.at[k, c, span], s_recv.at[k, slot, span],
            device_id=member(c), device_id_type=MESH,
        )

    def publish(k, span):
        for c in partners:
            stat_copy(k, span, c, me).start()
        for side, column in ((0, 0), (1, TILE - 1)):
            picked = raw[pl.ds(span * span_size + column, count, stride=TILE), :]
            edge_out[k, side, span] = picked.astype(jnp.bfloat16)

            @pl.when(has[side])
            def _():
                edge_copy(k, side, span, 1 - side).start()

        stat_in[k, me, span] = stat_out[k, span]

    def receive(k, span):
        for c in partners:
            stat_copy(k, span, c, c).wait_recv()
        for side in (0, 1):

            @pl.when(has[side])
            def _():
                edge_copy(k, side, span, side).wait_recv()

    def group_sum(t):
        lane = lax.broadcasted_iota(jnp.int32, t.shape, 1)
        width = t.shape[1]
        size = 1
        while size < width // GROUPS:
            up = pltpu.roll(t, width - size, 1)
            down = pltpu.roll(t, size, 1)
            t = t + jnp.where(lax.rem(lane // size, 2) == 0, up, down)
            size *= 2
        return t

    members = frames_here * height * TILE * group * (channels // GROUPS)

    def normalize_span(k, span):
        block = k // 2
        which = lax.rem(k, 2)
        total = stat_in[k, 0, span]
        for c in range(1, group):
            total = total + stat_in[k, c, span]
        total = group_sum(jnp.concatenate([total] * 4, axis=0))
        average = total[0:1] / members
        squares = total[1:2] / members
        inverse = lax.rsqrt(squares - average * average + EPS)
        params = gbuf[block]
        gain = jnp.where(which == 0, params[0:1], params[2:3])
        bias = jnp.where(which == 0, params[1:2], params[3:4])
        scale = inverse * gain

        def active(u):
            y = (u - average) * scale + bias
            return 0.5 * y * (1.0 + jnp.tanh(0.5 * y))

        flat = padded.reshape(lines * 2 * TILE, channels)
        for side, column in ((0, 7), (1, 8 + TILE)):

            @pl.when(has[side])
            def _():
                u = edge_in[k, side, span].astype(jnp.float32)
                flat[pl.ds(span * count * 2 * TILE + column, count, stride=2 * TILE), :] = active(u)

        for f in range(frames_here):
            frame = span * frames_here + f
            u = raw[pl.ds(frame * height * TILE, height * TILE)]
            here = pl.ds(frame * height, height)
            y = active(u).reshape(height, TILE, channels)
            padded[here, 8 : 8 + TILE] = y
            for dx in range(3):
                shifted = y if dx == 1 else padded[here, 7 + dx : 7 + dx + TILE]
                act[frame + 2, 1 : height + 1, :, dx * channels : (dx + 1) * channels] = (
                    shifted.astype(jnp.bfloat16)
                )

    def convolve_span(k, span):
        total = None
        for dt in range(3):
            columns = [
                act[pl.ds(span * frames_here + dt, frames_here), dy : dy + height].reshape(
                    span_size, 3 * channels
                )
                for dy in range(3)
            ]
            x = jnp.concatenate(columns, axis=1)
            w = wbuf[k, dt * (taps // 3) : (dt + 1) * (taps // 3)]
            part = jnp.dot(x, w, preferred_element_type=jnp.float32)
            total = part if total is None else total + part
        return total

    def feed(k):
        @pl.when(k <= 2)
        def _():
            pump(k)

        @pl.when(jnp.logical_and(k >= 2, k + 1 < convs))
        def _():
            pump(k + 1)

    def output_copy(c, sender, span):
        src = vin.at[
            pl.ds(span * frames_here, frames_here), pl.ds((c // cores) * rows_here, rows_here)
        ]
        return src, out.at[:, :, pl.ds(sender * TILE, TILE)]

    def finish(span):
        for c in partners:

            @pl.when(lax.rem(c, cores) == span)
            def _():
                src, dst = output_copy(c, me, span)
                pltpu.make_async_remote_copy(
                    src, dst, o_send.at[c], o_recv.at[me],
                    device_id=member(c), device_id_type=MESH,
                ).start()

        @pl.when(core == span)
        def _():
            src, dst = output_copy(me, me, span)
            pltpu.make_async_copy(src, dst, own_sem).start()

    for c in partners:
        src, dst = input_copy(me, c)
        pltpu.make_async_remote_copy(
            src, dst, in_send.at[c], in_recv.at[c], device_id=member(c), device_id_type=MESH
        ).wait_recv()
    own.wait()
    for span in range(cores):
        fresh = vin[span * frames_here : (span + 1) * frames_here]
        fresh = fresh.reshape(span_size, channels).astype(jnp.float32)
        values[span * span_size : (span + 1) * span_size] = fresh
        put(0, span, fresh)
        publish(0, span)
    for s in others:
        pltpu.make_async_remote_copy(
            small, gbuf.at[s], g_send.at[s], g_recv.at[s],
            device_id={"segment": s}, device_id_type=MESH,
        ).wait_recv()

    @pl.loop(0, segments)
    def _(block):
        k = 2 * block
        feed(k)
        for span in range(cores):
            receive(k, span)
            normalize_span(k, span)
            if span == 0:
                arrive(k)
            hidden = convolve_span(k, span)
            put(k + 1, span, hidden.astype(jnp.bfloat16).astype(jnp.float32))
            publish(k + 1, span)
        feed(k + 1)
        for span in range(cores):
            receive(k + 1, span)
            normalize_span(k + 1, span)
            if span == 0:
                arrive(k + 1)
            here = pl.ds(span * span_size, span_size)
            fresh = values[here] + convolve_span(k + 1, span)
            fresh = fresh.astype(jnp.bfloat16)
            values[here] = fresh.astype(jnp.float32)
            vin[pl.ds(span * frames_here, frames_here)] = fresh.reshape(
                frames_here, height, TILE, channels
            )

            @pl.when(block < segments - 1)
            def _():
                put(k + 2, span, values[here])
                publish(k + 2, span)

            @pl.when(block == segments - 1)
            def _():
                finish(span)

    for c in partners:
        src, dst = input_copy(c, me)
        pltpu.make_async_remote_copy(
            src, dst, in_send.at[c], in_recv.at[me], device_id=member(c), device_id_type=MESH
        ).wait_send()
    for s in others:
        pltpu.make_async_remote_copy(
            small, gbuf.at[seg], g_send.at[s], g_recv.at[seg],
            device_id={"segment": s}, device_id_type=MESH,
        ).wait_send()
    for i, source in enumerate((first, second)):
        k = 2 * seg + i
        for q in range(PIECES):
            rows = pl.ds(core * half + q * piece, piece)
            for slot, target in enumerate((across, along)):
                pltpu.make_async_remote_copy(
                    source.at[rows], wbuf.at[k, rows],
                    w_send.at[k, q, slot], w_recv.at[k, core, q],
                    device_id={"segment": target}, device_id_type=MESH,
                ).wait_send()

    @pl.loop(0, convs)
    def _(k):
        kind = relation(k)
        for q in range(PIECES):

            @pl.when(kind != 0)
            def _():
                landed(k, core, q).wait_send()

            @pl.when(kind == core + 1)
            def _():
                forwarded(k, q).wait_send()

        for span in range(cores):
            for c in partners:
                stat_copy(k, span, c, me).wait_send()
            for side in (0, 1):

                @pl.when(has[side])
                def _():
                    edge_copy(k, side, span, 1 - side).wait_send()

    src, dst = output_copy(me, me, core)
    pltpu.make_async_copy(src, dst, own_sem).wait()
    for c in partners:
        src, dst = output_copy(me, c, core)
        pltpu.make_async_remote_copy(
            src, dst, o_send.at[c], o_recv.at[c], device_id=member(c), device_id_type=MESH
        ).wait_recv()
        src, dst = output_copy(c, me, lax.rem(c, cores))
        pltpu.make_async_remote_copy(
            src, dst, o_send.at[c], o_recv.at[me], device_id=member(c), device_id_type=MESH
        ).wait_send()


def in_one_kernel(
    latents, conv_first, conv_second, gain_first, bias_first, gain_second, bias_second
):
    segments = lax.axis_size("segment")
    cores = lax.axis_size("tm")
    group = lax.axis_size("rows") * cores
    micro, frames_here, rows_here, columns, channels = latents.shape
    frames, height = frames_here * cores, rows_here * lax.axis_size("rows")
    lines, pixels = frames * height, frames * height * TILE
    convs = 2 * segments
    taps = 27 * channels
    small = jnp.concatenate([gain_first, bias_first, gain_second, bias_second])
    small = jnp.pad(small.astype(jnp.float32), ((0, 4), (0, 0)))
    dma = pltpu.SemaphoreType.DMA
    any_space = pl.BlockSpec(memory_space=pl.ANY)
    vmem = pl.BlockSpec(memory_space=pltpu.VMEM)
    result = pl.pallas_call(
        fused,
        out_shape=jax.ShapeDtypeStruct((frames_here, rows_here, columns, channels), jnp.bfloat16),
        in_specs=[any_space] * 3 + [vmem],
        out_specs=any_space,
        scratch_shapes=[
            pltpu.VMEM((convs, taps, channels), jnp.bfloat16),
            pltpu.VMEM((segments, 8, channels), jnp.float32),
            pltpu.VMEM((frames, height, TILE, channels), jnp.bfloat16),
            pltpu.VMEM((pixels, channels), jnp.float32),
            pltpu.VMEM((pixels, channels), jnp.float32),
            pltpu.VMEM((lines, 2 * TILE, channels), jnp.float32),
            pltpu.VMEM((frames + 2, height + 2, TILE, 3 * channels), jnp.bfloat16),
            pltpu.VMEM((convs, 2, cores, lines // cores, channels), jnp.bfloat16),
            pltpu.VMEM((convs, 2, cores, lines // cores, channels), jnp.bfloat16),
            pltpu.VMEM((convs, cores, 2, channels), jnp.float32),
            pltpu.VMEM((convs, group, cores, 2, channels), jnp.float32),
            dma((group,)), dma((group,)), dma,
            dma((convs, PIECES, 3)), dma((convs, 2, PIECES)), dma((2,)),
            dma((segments,)), dma((segments,)),
            dma((convs, 2, cores)), dma((convs, 2, cores)),
            dma((convs, group, cores)), dma((convs, group, cores)),
            dma((group,)), dma((group,)),
        ],
        compiler_params=pltpu.CompilerParams(
            collective_id=0, has_side_effects=True, vmem_limit_bytes=40 * 1024 * 1024
        ),
        cost_estimate=pl.CostEstimate(
            flops=2 * convs * pixels * taps * channels,
            bytes_accessed=6 * taps * channels,
            transcendentals=convs * pixels * channels,
        ),
    )(latents, conv_first.reshape(taps, channels), conv_second.reshape(taps, channels), small)
    return result[None]


def choose(latents, *params):
    cores = lax.axis_size("tm")
    group = lax.axis_size("rows") * cores
    fits = (
        lax.axis_size("segment") == 4
        and latents.shape[0] == 4
        and cores == 2
        and latents.shape[3] == group * TILE
    )
    return in_one_kernel(latents, *params) if fits else body(latents, *params)


def solution(mesh):
    in_specs = (
        P(None, "tm", "rows", None, None),
        P("segment", None, None, None, None, None),
        P("segment", None, None, None, None, None),
        P("segment", None),
        P("segment", None),
        P("segment", None),
        P("segment", None),
    )
    out_specs = P("segment", "tm", "rows", None, None)
    return jax.shard_map(choose, mesh=mesh, in_specs=in_specs, out_specs=out_specs, check_vma=False)
```

```python
import functools

import jax
import jax.numpy as jnp
from jax import lax
from jax.experimental import pallas as pl
from jax.experimental.pallas import tpu as pltpu
from jax.sharding import PartitionSpec as P

GROUPS = 32


EPS = 1e-06


def passed_along(value, axis, steps):
    count = lax.axis_size(axis)
    initial, last = (max(0, -steps), min(count, count - steps))
    return lax.ppermute(value, axis, [(source, source + steps) for source in range(initial, last)])


def padded_2(block, sides, width):
    for axis, dim in sides:
        count = lax.axis_size(axis)
        forward = [(i, i + 1) for i in range(count - 1)]
        backward = [(target, source) for source, target in forward]
        low = lax.ppermute(
            lax.slice_in_dim(block, block.shape[dim] - width, None, axis=dim), axis, forward
        )
        high = lax.ppermute(lax.slice_in_dim(block, 0, width, axis=dim), axis, backward)
        block = jnp.concatenate([low, block, high], axis=dim)
    return block


def normalize(values, norm_gain, norm_bias):
    frames, rows_here, columns, channels = values.shape
    width_group = channels // GROUPS
    grouped = values.astype(jnp.float32).reshape(frames, rows_here, columns, GROUPS, width_group)
    totals = lax.psum(
        (jnp.sum(grouped, axis=(0, 1, 2, 4)), jnp.sum(grouped * grouped, axis=(0, 1, 2, 4))), "rows"
    )
    members = frames * rows_here * lax.axis_size("rows") * columns * width_group
    average = totals[0] / members
    squares = totals[1] / members
    inverse = lax.rsqrt(squares - average * average + EPS)
    scaled = (grouped - average[:, None]) * inverse[:, None]
    scaled = scaled.reshape(values.shape) * norm_gain.astype(jnp.float32) + norm_bias.astype(
        jnp.float32
    )
    return jax.nn.silu(scaled).astype(jnp.bfloat16)


def convolve(active, kernel):
    previous = passed_along(active[-2:], "tm", 1)
    extended = jnp.concatenate([previous, active], axis=0)
    padded = padded_2(extended, (("rows", 1),), 1)
    padded = jnp.pad(padded, ((0, 0), (0, 0), (1, 1), (0, 0)))
    result = lax.conv_general_dilated(
        padded[None],
        kernel,
        (1, 1, 1),
        "VALID",
        dimension_numbers=("NDHWC", "DHWIO", "NDHWC"),
        preferred_element_type=jnp.float32,
    )
    return result[0]


def residual_block(values, params):
    first, second, gain_one, bias_one, gain_two, bias_two = params
    active = normalize(values, gain_one, bias_one)
    hidden = convolve(active, first).astype(jnp.bfloat16)
    active = normalize(hidden, gain_two, bias_two)
    return (values.astype(jnp.float32) + convolve(active, second)).astype(jnp.bfloat16)


def body(latents, conv_first, conv_second, gain_first, bias_first, gain_second, bias_second):
    segments = lax.axis_size("segment")
    micro = latents.shape[0]
    per_segment = micro // segments
    position = lax.axis_index("segment")
    small = jnp.stack([gain_first, bias_first, gain_second, bias_second], axis=1)
    small = lax.all_gather(small, "segment", axis=0, tiled=True)
    first = lax.all_gather(conv_first, "segment", axis=0, tiled=True)
    second = lax.all_gather(conv_second, "segment", axis=0, tiled=True)
    outs = []
    for index in range(per_segment):
        values = lax.dynamic_index_in_dim(
            latents, position * per_segment + index, 0, keepdims=False
        )
        for layer in range(first.shape[0]):
            gains = small[layer]
            values = residual_block(
                values, (first[layer], second[layer], gains[0], gains[1], gains[2], gains[3])
            )
        outs.append(values)
    return jnp.stack(outs)


MESH = pl.DeviceIdType.MESH
TILE = 16
PIECES = 3


def fused(
    latents, first, second, small, out,
    wbuf, gbuf, vin, values, raw, padded, act, edge_out, edge_in, stat_out, stat_in,
    in_send, in_recv, own_sem, w_send, w_recv, w_own, g_send, g_recv,
    e_send, e_recv, s_send, s_recv, o_send, o_recv,
):
    rows_count = lax.axis_size("rows")
    cores = lax.axis_size("tm")
    group = rows_count * cores
    segments = lax.axis_size("segment")
    z = lax.axis_index("rows")
    core = lax.axis_index("tm")
    seg = lax.axis_index("segment")
    me = z * cores + core
    _, frames_here, rows_here, _, channels = latents.shape
    frames = frames_here * cores
    height = rows_here * rows_count
    lines = frames * height
    taps = first.shape[0]
    half = taps // 2
    piece = half // PIECES
    span_size = frames_here * height * TILE
    convs = 2 * segments
    across = seg + 1 - 2 * lax.rem(seg, 2)
    along = lax.rem(seg + 2, 4)

    def member(c):
        return {"rows": c // cores, "tm": lax.rem(c, cores)}

    order = sorted(range(1, group), key=lambda d: -min(d, group - d))
    partners = [lax.rem(me + d, group) for d in order]
    others = [lax.rem(seg + d, segments) for d in range(1, segments)]

    barrier = pltpu.get_barrier_semaphore()
    for c in partners:
        pl.semaphore_signal(barrier, inc=1, device_id=member(c), device_id_type=MESH)
    for s in others:
        pl.semaphore_signal(barrier, inc=1, device_id={"segment": s}, device_id_type=MESH)
    pl.semaphore_wait(barrier, group - 1 + segments - 1)

    def start_owner(i, slot):
        k = 2 * seg + i
        for q in range(PIECES):
            rows = pl.ds(core * half + q * piece, piece)
            pltpu.make_async_remote_copy(
                (first, second)[i].at[rows], wbuf.at[k, rows],
                w_send.at[k, q, slot], w_recv.at[k, core, q],
                device_id={"segment": (across, along)[slot]}, device_id_type=MESH,
            ).start()

    late = (seg == 2, seg == 1)
    last = seg == segments - 1

    for slot in (0, 1):

        @pl.when(jnp.logical_not(late[slot]))
        def _():
            start_owner(0, slot)

    def input_copy(c, sender):
        dst = vin.at[
            pl.ds(lax.rem(sender, cores) * frames_here, frames_here),
            pl.ds((sender // cores) * rows_here, rows_here),
        ]
        src = latents.at[seg, :, :, pl.ds(c * TILE, TILE)]
        return src, dst

    for c in partners:
        src, dst = input_copy(c, me)
        pltpu.make_async_remote_copy(
            src, dst, in_send.at[c], in_recv.at[me], device_id=member(c), device_id_type=MESH
        ).start()
    src, dst = input_copy(me, me)
    own = pltpu.make_async_copy(src, dst, own_sem)
    own.start()

    for s in others:
        pltpu.make_async_remote_copy(
            small, gbuf.at[seg], g_send.at[s], g_recv.at[seg],
            device_id={"segment": s}, device_id_type=MESH,
        ).start()
    gbuf[seg] = small[...]

    for i, source in enumerate((first, second)):
        pltpu.make_async_copy(source, wbuf.at[2 * seg + i], w_own.at[i]).start()
    for slot in (0, 1):

        @pl.when(jnp.logical_not(jnp.logical_or(late[slot], last)))
        def _():
            start_owner(1, slot)


    act[...] = jnp.zeros_like(act)
    padded[...] = jnp.zeros_like(padded)

    def relation(k):
        block = k // 2
        low = lax.rem(lax.rem(seg, 2) + lax.rem(block, 2), 2)
        high = lax.rem(seg // 2 + block // 2, 2)
        return low + 2 * high

    def landed(k, part, q):
        rows = pl.ds(part * half + q * piece, piece)
        return pltpu.make_async_remote_copy(
            wbuf.at[k, rows], wbuf.at[k, rows], w_send.at[k, q, 2], w_recv.at[k, part, q],
            device_id={"tm": 1 - core}, device_id_type=MESH,
        )

    def forwarded(k, q):
        rows = pl.ds(core * half + q * piece, piece)
        target = jnp.where(core == 0, along, across)
        return pltpu.make_async_remote_copy(
            wbuf.at[k, rows], wbuf.at[k, rows], w_send.at[k, q, 0], w_recv.at[k, core, q],
            device_id={"segment": target}, device_id_type=MESH,
        )

    def pump(k):
        kind = relation(k)
        for q in range(PIECES):

            @pl.when(kind != 0)
            def _():
                landed(k, core, q).wait_recv()

                @pl.when(kind == core + 1)
                def _():
                    forwarded(k, q).start()

                landed(k, core, q).start()

    def arrive(k):
        kind = relation(k)

        @pl.when(kind != 0)
        def _():
            for q in range(PIECES):
                landed(k, 1 - core, q).wait_recv()

        @pl.when(kind == 0)
        def _():
            i = lax.rem(k, 2)
            pltpu.make_async_copy(first, wbuf.at[k], w_own.at[i]).wait()

    def put(k, span, fresh):
        raw[pl.ds(span * span_size, span_size)] = fresh
        total = jnp.sum(fresh, axis=0, keepdims=True)
        squares = jnp.sum(fresh * fresh, axis=0, keepdims=True)
        stat_out[k, span] = jnp.concatenate([total, squares], axis=0)

    count = frames_here * height

    def edge_copy(k, side, span, landing):
        return pltpu.make_async_remote_copy(
            edge_out.at[k, side, span], edge_in.at[k, landing, span],
            e_send.at[k, side, span], e_recv.at[k, landing, span],
            device_id=member(me - 1 if side == 0 else me + 1), device_id_type=MESH,
        )

    has = (me > 0, me < group - 1)

    def stat_copy(k, span, c, slot):
        return pltpu.make_async_remote_copy(
            stat_out.at[k, span], stat_in.at[k, slot, span],
            s_send.at[k, c, span], s_recv.at[k, slot, span],
            device_id=member(c), device_id_type=MESH,
        )

    def publish(k, span):
        for c in partners:
            stat_copy(k, span, c, me).start()
        for side, column in ((0, 0), (1, TILE - 1)):
            picked = raw[pl.ds(span * span_size + column, count, stride=TILE), :]
            edge_out[k, side, span] = picked.astype(jnp.bfloat16)

            @pl.when(has[side])
            def _():
                edge_copy(k, side, span, 1 - side).start()

        stat_in[k, me, span] = stat_out[k, span]

    def receive(k, span):
        for c in partners:
            stat_copy(k, span, c, c).wait_recv()
        for side in (0, 1):

            @pl.when(has[side])
            def _():
                edge_copy(k, side, span, side).wait_recv()

    def group_sum(t):
        lane = lax.broadcasted_iota(jnp.int32, t.shape, 1)
        width = t.shape[1]
        size = 1
        while size < width // GROUPS:
            up = pltpu.roll(t, width - size, 1)
            down = pltpu.roll(t, size, 1)
            t = t + jnp.where(lax.rem(lane // size, 2) == 0, up, down)
            size *= 2
        return t

    members = frames_here * height * TILE * group * (channels // GROUPS)

    def normalize_span(k, span):
        block = k // 2
        which = lax.rem(k, 2)
        total = stat_in[k, 0, span]
        for c in range(1, group):
            total = total + stat_in[k, c, span]
        total = group_sum(jnp.concatenate([total] * 4, axis=0))
        average = total[0:1] / members
        squares = total[1:2] / members
        inverse = lax.rsqrt(squares - average * average + EPS)
        params = gbuf[block]
        gain = jnp.where(which == 0, params[0:1], params[2:3])
        bias = jnp.where(which == 0, params[1:2], params[3:4])
        scale = inverse * gain

        def active(u):
            y = (u - average) * scale + bias
            return 0.5 * y * (1.0 + jnp.tanh(0.5 * y))

        flat = padded.reshape(lines * 2 * TILE, channels)
        for side, column in ((0, 7), (1, 8 + TILE)):

            @pl.when(has[side])
            def _():
                u = edge_in[k, side, span].astype(jnp.float32)
                flat[pl.ds(span * count * 2 * TILE + column, count, stride=2 * TILE), :] = active(u)

        for f in range(frames_here):
            frame = span * frames_here + f
            u = raw[pl.ds(frame * height * TILE, height * TILE)]
            here = pl.ds(frame * height, height)
            y = active(u).reshape(height, TILE, channels)
            padded[here, 8 : 8 + TILE] = y
            for dx in range(3):
                shifted = y if dx == 1 else padded[here, 7 + dx : 7 + dx + TILE]
                act[frame + 2, 1 : height + 1, :, dx * channels : (dx + 1) * channels] = (
                    shifted.astype(jnp.bfloat16)
                )

    def convolve_span(k, span):
        total = None
        for dt in range(3):
            columns = [
                act[pl.ds(span * frames_here + dt, frames_here), dy : dy + height].reshape(
                    span_size, 3 * channels
                )
                for dy in range(3)
            ]
            x = jnp.concatenate(columns, axis=1)
            w = wbuf[k, dt * (taps // 3) : (dt + 1) * (taps // 3)]
            part = jnp.dot(x, w, preferred_element_type=jnp.float32)
            total = part if total is None else total + part
        return total

    ahead = jnp.where(core == 0, across, along)

    def feed(k):
        @pl.when(k <= 1)
        def _():
            pump(k)

        for slot in (0, 1):

            @pl.when(jnp.logical_and(k == 0, late[slot]))
            def _():
                start_owner(0, slot)

            @pl.when(jnp.logical_and(k == 1, jnp.logical_or(late[slot], last)))
            def _():
                start_owner(1, slot)

        @pl.when(jnp.logical_and(jnp.logical_or(k == 1, k == 2), ahead != 0))
        def _():
            pump(2 * ahead + k - 1)

        @pl.when(jnp.logical_and(k == 2, ahead != 1))
        def _():
            pump(k)

        @pl.when(jnp.logical_and(jnp.logical_and(k >= 2, k + 1 < convs), (k + 1) // 2 != ahead))
        def _():
            pump(k + 1)

    def output_copy(c, sender, span):
        src = vin.at[
            pl.ds(span * frames_here, frames_here), pl.ds((c // cores) * rows_here, rows_here)
        ]
        return src, out.at[:, :, pl.ds(sender * TILE, TILE)]

    def finish(span):
        for c in partners:

            @pl.when(lax.rem(c, cores) == span)
            def _():
                src, dst = output_copy(c, me, span)
                pltpu.make_async_remote_copy(
                    src, dst, o_send.at[c], o_recv.at[me],
                    device_id=member(c), device_id_type=MESH,
                ).start()

        @pl.when(core == span)
        def _():
            src, dst = output_copy(me, me, span)
            pltpu.make_async_copy(src, dst, own_sem).start()

    for c in partners:
        src, dst = input_copy(me, c)
        pltpu.make_async_remote_copy(
            src, dst, in_send.at[c], in_recv.at[c], device_id=member(c), device_id_type=MESH
        ).wait_recv()
    own.wait()
    for span in range(cores):
        fresh = vin[span * frames_here : (span + 1) * frames_here]
        fresh = fresh.reshape(span_size, channels).astype(jnp.float32)
        values[span * span_size : (span + 1) * span_size] = fresh
        put(0, span, fresh)
        publish(0, span)
    for s in others:
        pltpu.make_async_remote_copy(
            small, gbuf.at[s], g_send.at[s], g_recv.at[s],
            device_id={"segment": s}, device_id_type=MESH,
        ).wait_recv()

    @pl.loop(0, segments)
    def _(block):
        k = 2 * block
        feed(k)
        for span in range(cores):
            receive(k, span)
            normalize_span(k, span)
            if span == 0:
                arrive(k)
            hidden = convolve_span(k, span)
            put(k + 1, span, hidden.astype(jnp.bfloat16).astype(jnp.float32))
            publish(k + 1, span)
        feed(k + 1)
        for span in range(cores):
            receive(k + 1, span)
            normalize_span(k + 1, span)
            if span == 0:
                arrive(k + 1)
            here = pl.ds(span * span_size, span_size)
            fresh = values[here] + convolve_span(k + 1, span)
            fresh = fresh.astype(jnp.bfloat16)
            values[here] = fresh.astype(jnp.float32)
            vin[pl.ds(span * frames_here, frames_here)] = fresh.reshape(
                frames_here, height, TILE, channels
            )

            @pl.when(block < segments - 1)
            def _():
                put(k + 2, span, values[here])
                publish(k + 2, span)

            @pl.when(block == segments - 1)
            def _():
                finish(span)

    for c in partners:
        src, dst = input_copy(c, me)
        pltpu.make_async_remote_copy(
            src, dst, in_send.at[c], in_recv.at[me], device_id=member(c), device_id_type=MESH
        ).wait_send()
    for s in others:
        pltpu.make_async_remote_copy(
            small, gbuf.at[seg], g_send.at[s], g_recv.at[seg],
            device_id={"segment": s}, device_id_type=MESH,
        ).wait_send()
    for i, source in enumerate((first, second)):
        k = 2 * seg + i
        for q in range(PIECES):
            rows = pl.ds(core * half + q * piece, piece)
            for slot, target in enumerate((across, along)):
                pltpu.make_async_remote_copy(
                    source.at[rows], wbuf.at[k, rows],
                    w_send.at[k, q, slot], w_recv.at[k, core, q],
                    device_id={"segment": target}, device_id_type=MESH,
                ).wait_send()

    @pl.loop(0, convs)
    def _(k):
        kind = relation(k)
        for q in range(PIECES):

            @pl.when(kind != 0)
            def _():
                landed(k, core, q).wait_send()

            @pl.when(kind == core + 1)
            def _():
                forwarded(k, q).wait_send()

        for span in range(cores):
            for c in partners:
                stat_copy(k, span, c, me).wait_send()
            for side in (0, 1):

                @pl.when(has[side])
                def _():
                    edge_copy(k, side, span, 1 - side).wait_send()

    src, dst = output_copy(me, me, core)
    pltpu.make_async_copy(src, dst, own_sem).wait()
    for c in partners:
        src, dst = output_copy(me, c, core)
        pltpu.make_async_remote_copy(
            src, dst, o_send.at[c], o_recv.at[c], device_id=member(c), device_id_type=MESH
        ).wait_recv()
        src, dst = output_copy(c, me, lax.rem(c, cores))
        pltpu.make_async_remote_copy(
            src, dst, o_send.at[c], o_recv.at[me], device_id=member(c), device_id_type=MESH
        ).wait_send()


def in_one_kernel(
    latents, conv_first, conv_second, gain_first, bias_first, gain_second, bias_second
):
    segments = lax.axis_size("segment")
    cores = lax.axis_size("tm")
    group = lax.axis_size("rows") * cores
    micro, frames_here, rows_here, columns, channels = latents.shape
    frames, height = frames_here * cores, rows_here * lax.axis_size("rows")
    lines, pixels = frames * height, frames * height * TILE
    convs = 2 * segments
    taps = 27 * channels
    small = jnp.concatenate([gain_first, bias_first, gain_second, bias_second])
    small = jnp.pad(small.astype(jnp.float32), ((0, 4), (0, 0)))
    dma = pltpu.SemaphoreType.DMA
    any_space = pl.BlockSpec(memory_space=pl.ANY)
    vmem = pl.BlockSpec(memory_space=pltpu.VMEM)
    result = pl.pallas_call(
        fused,
        out_shape=jax.ShapeDtypeStruct((frames_here, rows_here, columns, channels), jnp.bfloat16),
        in_specs=[any_space] * 3 + [vmem],
        out_specs=any_space,
        scratch_shapes=[
            pltpu.VMEM((convs, taps, channels), jnp.bfloat16),
            pltpu.VMEM((segments, 8, channels), jnp.float32),
            pltpu.VMEM((frames, height, TILE, channels), jnp.bfloat16),
            pltpu.VMEM((pixels, channels), jnp.float32),
            pltpu.VMEM((pixels, channels), jnp.float32),
            pltpu.VMEM((lines, 2 * TILE, channels), jnp.float32),
            pltpu.VMEM((frames + 2, height + 2, TILE, 3 * channels), jnp.bfloat16),
            pltpu.VMEM((convs, 2, cores, lines // cores, channels), jnp.bfloat16),
            pltpu.VMEM((convs, 2, cores, lines // cores, channels), jnp.bfloat16),
            pltpu.VMEM((convs, cores, 2, channels), jnp.float32),
            pltpu.VMEM((convs, group, cores, 2, channels), jnp.float32),
            dma((group,)), dma((group,)), dma,
            dma((convs, PIECES, 3)), dma((convs, 2, PIECES)), dma((2,)),
            dma((segments,)), dma((segments,)),
            dma((convs, 2, cores)), dma((convs, 2, cores)),
            dma((convs, group, cores)), dma((convs, group, cores)),
            dma((group,)), dma((group,)),
        ],
        compiler_params=pltpu.CompilerParams(
            collective_id=0, has_side_effects=True, vmem_limit_bytes=40 * 1024 * 1024
        ),
        cost_estimate=pl.CostEstimate(
            flops=2 * convs * pixels * taps * channels,
            bytes_accessed=6 * taps * channels,
            transcendentals=convs * pixels * channels,
        ),
    )(latents, conv_first.reshape(taps, channels), conv_second.reshape(taps, channels), small)
    return result[None]


def choose(latents, *params):
    cores = lax.axis_size("tm")
    group = lax.axis_size("rows") * cores
    fits = (
        lax.axis_size("segment") == 4
        and latents.shape[0] == 4
        and cores == 2
        and latents.shape[3] == group * TILE
    )
    return in_one_kernel(latents, *params) if fits else body(latents, *params)


def solution(mesh):
    in_specs = (
        P(None, "tm", "rows", None, None),
        P("segment", None, None, None, None, None),
        P("segment", None, None, None, None, None),
        P("segment", None),
        P("segment", None),
        P("segment", None),
        P("segment", None),
    )
    out_specs = P("segment", "tm", "rows", None, None)
    return jax.shard_map(choose, mesh=mesh, in_specs=in_specs, out_specs=out_specs, check_vma=False)
```

```python
import functools

import jax
import jax.numpy as jnp
from jax import lax
from jax.experimental import pallas as pl
from jax.experimental.pallas import tpu as pltpu
from jax.sharding import PartitionSpec as P

GROUPS = 32


EPS = 1e-06


def passed_along(value, axis, steps):
    count = lax.axis_size(axis)
    initial, last = (max(0, -steps), min(count, count - steps))
    return lax.ppermute(value, axis, [(source, source + steps) for source in range(initial, last)])


def padded_2(block, sides, width):
    for axis, dim in sides:
        count = lax.axis_size(axis)
        forward = [(i, i + 1) for i in range(count - 1)]
        backward = [(target, source) for source, target in forward]
        low = lax.ppermute(
            lax.slice_in_dim(block, block.shape[dim] - width, None, axis=dim), axis, forward
        )
        high = lax.ppermute(lax.slice_in_dim(block, 0, width, axis=dim), axis, backward)
        block = jnp.concatenate([low, block, high], axis=dim)
    return block


def normalize(values, norm_gain, norm_bias):
    frames, rows_here, columns, channels = values.shape
    width_group = channels // GROUPS
    grouped = values.astype(jnp.float32).reshape(frames, rows_here, columns, GROUPS, width_group)
    totals = lax.psum(
        (jnp.sum(grouped, axis=(0, 1, 2, 4)), jnp.sum(grouped * grouped, axis=(0, 1, 2, 4))), "rows"
    )
    members = frames * rows_here * lax.axis_size("rows") * columns * width_group
    average = totals[0] / members
    squares = totals[1] / members
    inverse = lax.rsqrt(squares - average * average + EPS)
    scaled = (grouped - average[:, None]) * inverse[:, None]
    scaled = scaled.reshape(values.shape) * norm_gain.astype(jnp.float32) + norm_bias.astype(
        jnp.float32
    )
    return jax.nn.silu(scaled).astype(jnp.bfloat16)


def convolve(active, kernel):
    previous = passed_along(active[-2:], "tm", 1)
    extended = jnp.concatenate([previous, active], axis=0)
    padded = padded_2(extended, (("rows", 1),), 1)
    padded = jnp.pad(padded, ((0, 0), (0, 0), (1, 1), (0, 0)))
    result = lax.conv_general_dilated(
        padded[None],
        kernel,
        (1, 1, 1),
        "VALID",
        dimension_numbers=("NDHWC", "DHWIO", "NDHWC"),
        preferred_element_type=jnp.float32,
    )
    return result[0]


def residual_block(values, params):
    first, second, gain_one, bias_one, gain_two, bias_two = params
    active = normalize(values, gain_one, bias_one)
    hidden = convolve(active, first).astype(jnp.bfloat16)
    active = normalize(hidden, gain_two, bias_two)
    return (values.astype(jnp.float32) + convolve(active, second)).astype(jnp.bfloat16)


def body(latents, conv_first, conv_second, gain_first, bias_first, gain_second, bias_second):
    segments = lax.axis_size("segment")
    micro = latents.shape[0]
    per_segment = micro // segments
    position = lax.axis_index("segment")
    small = jnp.stack([gain_first, bias_first, gain_second, bias_second], axis=1)
    small = lax.all_gather(small, "segment", axis=0, tiled=True)
    first = lax.all_gather(conv_first, "segment", axis=0, tiled=True)
    second = lax.all_gather(conv_second, "segment", axis=0, tiled=True)
    outs = []
    for index in range(per_segment):
        values = lax.dynamic_index_in_dim(
            latents, position * per_segment + index, 0, keepdims=False
        )
        for layer in range(first.shape[0]):
            gains = small[layer]
            values = residual_block(
                values, (first[layer], second[layer], gains[0], gains[1], gains[2], gains[3])
            )
        outs.append(values)
    return jnp.stack(outs)


MESH = pl.DeviceIdType.MESH
TILE = 16
PIECES = 3


def fused(
    latents, first, second, small, out,
    wbuf, gbuf, vin, values, raw, padded, act, edge_out, edge_in, stat_out, stat_in,
    in_send, in_recv, own_sem, w_send, w_recv, w_own, g_send, g_recv,
    e_send, e_recv, s_send, s_recv, o_send, o_recv,
):
    rows_count = lax.axis_size("rows")
    cores = lax.axis_size("tm")
    group = rows_count * cores
    segments = lax.axis_size("segment")
    z = lax.axis_index("rows")
    core = lax.axis_index("tm")
    seg = lax.axis_index("segment")
    me = z * cores + core
    _, frames_here, rows_here, _, channels = latents.shape
    frames = frames_here * cores
    height = rows_here * rows_count
    lines = frames * height
    taps = first.shape[0]
    half = taps // 2
    piece = half // PIECES
    span_size = frames_here * height * TILE
    convs = 2 * segments
    across = seg + 1 - 2 * lax.rem(seg, 2)
    along = lax.rem(seg + 2, 4)

    def member(c):
        return {"rows": c // cores, "tm": lax.rem(c, cores)}

    order = sorted(range(1, group), key=lambda d: -min(d, group - d))
    partners = [lax.rem(me + d, group) for d in order]
    others = [lax.rem(seg + d, segments) for d in range(1, segments)]

    barrier = pltpu.get_barrier_semaphore()
    for c in partners:
        pl.semaphore_signal(barrier, inc=1, device_id=member(c), device_id_type=MESH)
    for s in others:
        pl.semaphore_signal(barrier, inc=1, device_id={"segment": s}, device_id_type=MESH)
    pl.semaphore_wait(barrier, group - 1 + segments - 1)

    def start_owner(i, slot):
        k = 2 * seg + i
        for q in range(PIECES):
            rows = pl.ds(core * half + q * piece, piece)
            pltpu.make_async_remote_copy(
                (first, second)[i].at[rows], wbuf.at[k, rows],
                w_send.at[k, q, slot], w_recv.at[k, core, q],
                device_id={"segment": (across, along)[slot]}, device_id_type=MESH,
            ).start()

    for slot in (0, 1):
        start_owner(0, slot)

    def input_copy(c, sender):
        dst = vin.at[
            pl.ds(lax.rem(sender, cores) * frames_here, frames_here),
            pl.ds((sender // cores) * rows_here, rows_here),
        ]
        src = latents.at[seg, :, :, pl.ds(c * TILE, TILE)]
        return src, dst

    for c in partners:
        src, dst = input_copy(c, me)
        pltpu.make_async_remote_copy(
            src, dst, in_send.at[c], in_recv.at[me], device_id=member(c), device_id_type=MESH
        ).start()
    src, dst = input_copy(me, me)
    own = pltpu.make_async_copy(src, dst, own_sem)
    own.start()

    for s in others:
        pltpu.make_async_remote_copy(
            small, gbuf.at[seg], g_send.at[s], g_recv.at[seg],
            device_id={"segment": s}, device_id_type=MESH,
        ).start()
    gbuf[seg] = small[...]

    for i, source in enumerate((first, second)):
        pltpu.make_async_copy(source, wbuf.at[2 * seg + i], w_own.at[i]).start()
    for slot in (0, 1):
        start_owner(1, slot)

    act[...] = jnp.zeros_like(act)
    padded[...] = jnp.zeros_like(padded)

    def relation(k):
        block = k // 2
        low = lax.rem(lax.rem(seg, 2) + lax.rem(block, 2), 2)
        high = lax.rem(seg // 2 + block // 2, 2)
        return low + 2 * high

    def landed(k, part, q):
        rows = pl.ds(part * half + q * piece, piece)
        return pltpu.make_async_remote_copy(
            wbuf.at[k, rows], wbuf.at[k, rows], w_send.at[k, q, 2], w_recv.at[k, part, q],
            device_id={"tm": 1 - core}, device_id_type=MESH,
        )

    def forwarded(k, q):
        rows = pl.ds(core * half + q * piece, piece)
        target = jnp.where(core == 0, along, across)
        return pltpu.make_async_remote_copy(
            wbuf.at[k, rows], wbuf.at[k, rows], w_send.at[k, q, 0], w_recv.at[k, core, q],
            device_id={"segment": target}, device_id_type=MESH,
        )

    def pump(k):
        kind = relation(k)
        for q in range(PIECES):

            @pl.when(kind != 0)
            def _():
                landed(k, core, q).wait_recv()

                @pl.when(kind == core + 1)
                def _():
                    forwarded(k, q).start()

                landed(k, core, q).start()

    def arrive(k):
        kind = relation(k)

        @pl.when(kind != 0)
        def _():
            for q in range(PIECES):
                landed(k, 1 - core, q).wait_recv()

        @pl.when(kind == 0)
        def _():
            i = lax.rem(k, 2)
            pltpu.make_async_copy(first, wbuf.at[k], w_own.at[i]).wait()

    def put(k, span, fresh):
        raw[pl.ds(span * span_size, span_size)] = fresh
        total = jnp.sum(fresh, axis=0, keepdims=True)
        squares = jnp.sum(fresh * fresh, axis=0, keepdims=True)
        stat_out[k, span] = jnp.concatenate([total, squares], axis=0)

    count = frames_here * height

    def edge_copy(k, side, span, landing):
        return pltpu.make_async_remote_copy(
            edge_out.at[k, side, span], edge_in.at[k, landing, span],
            e_send.at[k, side, span], e_recv.at[k, landing, span],
            device_id=member(me - 1 if side == 0 else me + 1), device_id_type=MESH,
        )

    has = (me > 0, me < group - 1)

    def stat_copy(k, span, c, slot):
        return pltpu.make_async_remote_copy(
            stat_out.at[k, span], stat_in.at[k, slot, span],
            s_send.at[k, c, span], s_recv.at[k, slot, span],
            device_id=member(c), device_id_type=MESH,
        )

    def publish(k, span):
        for c in partners:
            stat_copy(k, span, c, me).start()
        for side, column in ((0, 0), (1, TILE - 1)):
            picked = raw[pl.ds(span * span_size + column, count, stride=TILE), :]
            edge_out[k, side, span] = picked.astype(jnp.bfloat16)

            @pl.when(has[side])
            def _():
                edge_copy(k, side, span, 1 - side).start()

        stat_in[k, me, span] = stat_out[k, span]

    def receive(k, span):
        for c in partners:
            stat_copy(k, span, c, c).wait_recv()
        for side in (0, 1):

            @pl.when(has[side])
            def _():
                edge_copy(k, side, span, side).wait_recv()

    def group_sum(t):
        lane = lax.broadcasted_iota(jnp.int32, t.shape, 1)
        width = t.shape[1]
        size = 1
        while size < width // GROUPS:
            up = pltpu.roll(t, width - size, 1)
            down = pltpu.roll(t, size, 1)
            t = t + jnp.where(lax.rem(lane // size, 2) == 0, up, down)
            size *= 2
        return t

    members = frames_here * height * TILE * group * (channels // GROUPS)

    def normalize_span(k, span):
        block = k // 2
        which = lax.rem(k, 2)
        total = stat_in[k, 0, span]
        for c in range(1, group):
            total = total + stat_in[k, c, span]
        total = group_sum(jnp.concatenate([total] * 4, axis=0))
        average = total[0:1] / members
        squares = total[1:2] / members
        inverse = lax.rsqrt(squares - average * average + EPS)
        params = gbuf[block]
        gain = jnp.where(which == 0, params[0:1], params[2:3])
        bias = jnp.where(which == 0, params[1:2], params[3:4])
        scale = inverse * gain

        def active(u):
            y = (u - average) * scale + bias
            return 0.5 * y * (1.0 + jnp.tanh(0.5 * y))

        flat = padded.reshape(lines * 2 * TILE, channels)
        for side, column in ((0, 7), (1, 8 + TILE)):

            @pl.when(has[side])
            def _():
                u = edge_in[k, side, span].astype(jnp.float32)
                flat[pl.ds(span * count * 2 * TILE + column, count, stride=2 * TILE), :] = active(u)

        for f in range(frames_here):
            frame = span * frames_here + f
            u = raw[pl.ds(frame * height * TILE, height * TILE)]
            here = pl.ds(frame * height, height)
            y = active(u).reshape(height, TILE, channels)
            padded[here, 8 : 8 + TILE] = y
            for dx in range(3):
                shifted = y if dx == 1 else padded[here, 7 + dx : 7 + dx + TILE]
                act[frame + 2, 1 : height + 1, :, dx * channels : (dx + 1) * channels] = (
                    shifted.astype(jnp.bfloat16)
                )

    def convolve_span(k, span):
        total = None
        for dt in range(3):
            columns = [
                act[pl.ds(span * frames_here + dt, frames_here), dy : dy + height].reshape(
                    span_size, 3 * channels
                )
                for dy in range(3)
            ]
            x = jnp.concatenate(columns, axis=1)
            w = wbuf[k, dt * (taps // 3) : (dt + 1) * (taps // 3)]
            part = jnp.dot(x, w, preferred_element_type=jnp.float32)
            total = part if total is None else total + part
        return total

    ahead = jnp.where(core == 0, across, along)

    def feed(k):
        @pl.when(k <= 1)
        def _():
            pump(k)

        @pl.when(jnp.logical_and(jnp.logical_or(k == 1, k == 2), ahead != 0))
        def _():
            pump(2 * ahead + k - 1)

        @pl.when(jnp.logical_and(k == 2, ahead != 1))
        def _():
            pump(k)

        @pl.when(jnp.logical_and(jnp.logical_and(k >= 2, k + 1 < convs), (k + 1) // 2 != ahead))
        def _():
            pump(k + 1)

    def output_copy(c, sender, span):
        src = vin.at[
            pl.ds(span * frames_here, frames_here), pl.ds((c // cores) * rows_here, rows_here)
        ]
        return src, out.at[:, :, pl.ds(sender * TILE, TILE)]

    def finish(span):
        for c in partners:

            @pl.when(lax.rem(c, cores) == span)
            def _():
                src, dst = output_copy(c, me, span)
                pltpu.make_async_remote_copy(
                    src, dst, o_send.at[c], o_recv.at[me],
                    device_id=member(c), device_id_type=MESH,
                ).start()

        @pl.when(core == span)
        def _():
            src, dst = output_copy(me, me, span)
            pltpu.make_async_copy(src, dst, own_sem).start()

    for c in partners:
        src, dst = input_copy(me, c)
        pltpu.make_async_remote_copy(
            src, dst, in_send.at[c], in_recv.at[c], device_id=member(c), device_id_type=MESH
        ).wait_recv()
    own.wait()
    for span in range(cores):
        fresh = vin[span * frames_here : (span + 1) * frames_here]
        fresh = fresh.reshape(span_size, channels).astype(jnp.float32)
        values[span * span_size : (span + 1) * span_size] = fresh
        put(0, span, fresh)
        publish(0, span)
    for s in others:
        pltpu.make_async_remote_copy(
            small, gbuf.at[s], g_send.at[s], g_recv.at[s],
            device_id={"segment": s}, device_id_type=MESH,
        ).wait_recv()

    @pl.loop(0, segments)
    def _(block):
        k = 2 * block
        feed(k)
        for span in range(cores):
            receive(k, span)
            normalize_span(k, span)
            if span == 0:
                arrive(k)
            hidden = convolve_span(k, span)
            put(k + 1, span, hidden.astype(jnp.bfloat16).astype(jnp.float32))
            publish(k + 1, span)
        feed(k + 1)
        for span in range(cores):
            receive(k + 1, span)
            normalize_span(k + 1, span)
            if span == 0:
                arrive(k + 1)
            here = pl.ds(span * span_size, span_size)
            fresh = values[here] + convolve_span(k + 1, span)
            fresh = fresh.astype(jnp.bfloat16)
            values[here] = fresh.astype(jnp.float32)
            vin[pl.ds(span * frames_here, frames_here)] = fresh.reshape(
                frames_here, height, TILE, channels
            )

            @pl.when(block < segments - 1)
            def _():
                put(k + 2, span, values[here])
                publish(k + 2, span)

            @pl.when(block == segments - 1)
            def _():
                finish(span)

    for c in partners:
        src, dst = input_copy(c, me)
        pltpu.make_async_remote_copy(
            src, dst, in_send.at[c], in_recv.at[me], device_id=member(c), device_id_type=MESH
        ).wait_send()
    for s in others:
        pltpu.make_async_remote_copy(
            small, gbuf.at[seg], g_send.at[s], g_recv.at[seg],
            device_id={"segment": s}, device_id_type=MESH,
        ).wait_send()
    for i, source in enumerate((first, second)):
        k = 2 * seg + i
        for q in range(PIECES):
            rows = pl.ds(core * half + q * piece, piece)
            for slot, target in enumerate((across, along)):
                pltpu.make_async_remote_copy(
                    source.at[rows], wbuf.at[k, rows],
                    w_send.at[k, q, slot], w_recv.at[k, core, q],
                    device_id={"segment": target}, device_id_type=MESH,
                ).wait_send()

    @pl.loop(0, convs)
    def _(k):
        kind = relation(k)
        for q in range(PIECES):

            @pl.when(kind != 0)
            def _():
                landed(k, core, q).wait_send()

            @pl.when(kind == core + 1)
            def _():
                forwarded(k, q).wait_send()

        for span in range(cores):
            for c in partners:
                stat_copy(k, span, c, me).wait_send()
            for side in (0, 1):

                @pl.when(has[side])
                def _():
                    edge_copy(k, side, span, 1 - side).wait_send()

    src, dst = output_copy(me, me, core)
    pltpu.make_async_copy(src, dst, own_sem).wait()
    for c in partners:
        src, dst = output_copy(me, c, core)
        pltpu.make_async_remote_copy(
            src, dst, o_send.at[c], o_recv.at[c], device_id=member(c), device_id_type=MESH
        ).wait_recv()
        src, dst = output_copy(c, me, lax.rem(c, cores))
        pltpu.make_async_remote_copy(
            src, dst, o_send.at[c], o_recv.at[me], device_id=member(c), device_id_type=MESH
        ).wait_send()


def in_one_kernel(
    latents, conv_first, conv_second, gain_first, bias_first, gain_second, bias_second
):
    segments = lax.axis_size("segment")
    cores = lax.axis_size("tm")
    group = lax.axis_size("rows") * cores
    micro, frames_here, rows_here, columns, channels = latents.shape
    frames, height = frames_here * cores, rows_here * lax.axis_size("rows")
    lines, pixels = frames * height, frames * height * TILE
    convs = 2 * segments
    taps = 27 * channels
    small = jnp.concatenate([gain_first, bias_first, gain_second, bias_second])
    small = jnp.pad(small.astype(jnp.float32), ((0, 4), (0, 0)))
    dma = pltpu.SemaphoreType.DMA
    any_space = pl.BlockSpec(memory_space=pl.ANY)
    vmem = pl.BlockSpec(memory_space=pltpu.VMEM)
    result = pl.pallas_call(
        fused,
        out_shape=jax.ShapeDtypeStruct((frames_here, rows_here, columns, channels), jnp.bfloat16),
        in_specs=[any_space] * 3 + [vmem],
        out_specs=any_space,
        scratch_shapes=[
            pltpu.VMEM((convs, taps, channels), jnp.bfloat16),
            pltpu.VMEM((segments, 8, channels), jnp.float32),
            pltpu.VMEM((frames, height, TILE, channels), jnp.bfloat16),
            pltpu.VMEM((pixels, channels), jnp.float32),
            pltpu.VMEM((pixels, channels), jnp.float32),
            pltpu.VMEM((lines, 2 * TILE, channels), jnp.float32),
            pltpu.VMEM((frames + 2, height + 2, TILE, 3 * channels), jnp.bfloat16),
            pltpu.VMEM((convs, 2, cores, lines // cores, channels), jnp.bfloat16),
            pltpu.VMEM((convs, 2, cores, lines // cores, channels), jnp.bfloat16),
            pltpu.VMEM((convs, cores, 2, channels), jnp.float32),
            pltpu.VMEM((convs, group, cores, 2, channels), jnp.float32),
            dma((group,)), dma((group,)), dma,
            dma((convs, PIECES, 3)), dma((convs, 2, PIECES)), dma((2,)),
            dma((segments,)), dma((segments,)),
            dma((convs, 2, cores)), dma((convs, 2, cores)),
            dma((convs, group, cores)), dma((convs, group, cores)),
            dma((group,)), dma((group,)),
        ],
        compiler_params=pltpu.CompilerParams(
            collective_id=0, has_side_effects=True, vmem_limit_bytes=40 * 1024 * 1024
        ),
        cost_estimate=pl.CostEstimate(
            flops=2 * convs * pixels * taps * channels,
            bytes_accessed=6 * taps * channels,
            transcendentals=convs * pixels * channels,
        ),
    )(latents, conv_first.reshape(taps, channels), conv_second.reshape(taps, channels), small)
    return result[None]


def choose(latents, *params):
    cores = lax.axis_size("tm")
    group = lax.axis_size("rows") * cores
    fits = (
        lax.axis_size("segment") == 4
        and latents.shape[0] == 4
        and cores == 2
        and latents.shape[3] == group * TILE
    )
    return in_one_kernel(latents, *params) if fits else body(latents, *params)


def solution(mesh):
    in_specs = (
        P(None, "tm", "rows", None, None),
        P("segment", None, None, None, None, None),
        P("segment", None, None, None, None, None),
        P("segment", None),
        P("segment", None),
        P("segment", None),
        P("segment", None),
    )
    out_specs = P("segment", "tm", "rows", None, None)
    return jax.shard_map(choose, mesh=mesh, in_specs=in_specs, out_specs=out_specs, check_vma=False)
```
